32 devices in a mesh: gx: 8 (over y, x, core), gy: 4 (over z).
Axes of the slice: x: 2, y: 2, z: 4, core: 2. Of those that a mesh axis runs over, the one named last changes fastest.
Arguments:
- positions: float32 [3, 32, 16, 256], P(None, 'gx', 'gy'), may hold values from 0 to 1
- velocity: float32 [3, 32, 16, 256], P(None, 'gx', 'gy'), may hold values from -3 to 3
- density: float32 [32, 16, 256], P('gx', 'gy'), may hold values from 0.7 to 1.3
- cell_fill: int32 [32, 16], P('gx', 'gy'), may hold values from 64 to 256
- pair_cells: int32 [8, 4, 2, 86], P('gx', 'gy'), may hold values from 0 to 35, as said below
- pair_counts: int32 [8, 4, 2], P('gx', 'gy'), may hold values from 0 to 86, as said below
- shell_nodes: int32 [4, 32, 16], P(None, 'gx', 'gy'), may hold values from 0 to 32767, as said below
- shell_weights: float32 [4, 32, 16], P(None, 'gx', 'gy'), may hold values from 0.2 to 1
- shell_links: int32 [4, 32768], P(None, 'gx'), may hold values from 0 to 4095
- shell_disp: float32 [3, 32768], P(None, 'gx'), may hold values from -3 to 3
- shell_vel: float32 [3, 32768], P(None, 'gx'), may hold values from -3 to 3
Outputs:
- fluid_velocity: float32 [3, 32, 16, 256], P(None, 'gx', 'gy')
- fluid_density: float32 [32, 16, 256], P('gx', 'gy')
- shell_speed: float32 [3, 32768], P(None, 'gx')
- shell_offset: float32 [3, 32768], P(None, 'gx')
The draws below stay inside these ranges and needn't reach their ends.
Inputs may be any that keep to these rules, and one draw needn't show every extreme that they name: pair_cells[i, j, 0, s] and pair_cells[i, j, 1, s] are row-major flat indices into the (6) x (6) block of device (i, j) extended by one cell on each side; below pair_counts[i, j, 1] they name two distinct neighbouring cells (8-neighbourhood), the first inside the block, the second inside the grid, no unordered pair twice; a pair inside one block is listed by that device only, below pair_counts[i, j, 0]; a pair of cells on two devices is listed by both, below pair_counts[.., 0] on exactly one of them. pair_counts[i, j, 0] <= pair_counts[i, j, 1]. `shell_nodes`: a cell in cell columns x * 4 to (x + 1) * 4 - 1 is tied only to nodes of strips x - 1, x and x + 1, strip x holding nodes x * 4096 to (x + 1) * 4096 - 1.
All inputs are finite; a program needn't handle non-finite values.
Results may differ from the reference program's by a relative error of at most 0.0001.
Values sent between devices are 32-bit elements; how exact they have to be, the bound alone decides.
A program may use at most 64 MiB of HBM per device.

```python
import jax
import jax.numpy as jnp
from jax import lax

CELL = 256
CXL = 4
CYL = 4
NS_STRIP = 4096
MAPN = 4
LINKS = 4
SUBSTEPS = 2
NXC = 32
NYC = 16
NS = 32768
PAIR_SLOTS = 86
N_GX = 8
N_GY = 4


def pair_tables(key):
    count_x = NXC // CXL
    count_y = NYC // CYL
    roll_live = jax.random.randint(jax.random.fold_in(key, 11), (NXC, NYC, 4), 0, 100)
    roll_owner = jax.random.randint(jax.random.fold_in(key, 12), (NXC, NYC, 4), 0, 2)
    deep_half = jnp.arange(NXC, dtype=jnp.int32)[:, None, None] < NXC // 2
    alive_table = roll_live < jnp.where(deep_half, 100, 50)
    step_x = jnp.array([1, 0, 1, 1, -1, 0, -1, -1], jnp.int32)
    step_y = jnp.array([0, 1, 1, -1, 0, -1, -1, 1], jnp.int32)
    shape = (CXL, CYL, 8)
    forward = jnp.broadcast_to(jnp.arange(8) < 4, shape)
    direction = jnp.broadcast_to(jnp.arange(8, dtype=jnp.int32) % 4, shape)
    local_x = jnp.broadcast_to(jnp.arange(CXL, dtype=jnp.int32)[:, None, None], shape)
    local_y = jnp.broadcast_to(jnp.arange(CYL, dtype=jnp.int32)[None, :, None], shape)
    near_x = local_x + step_x
    near_y = local_y + step_y
    in_block = (near_x >= 0) & (near_x < CXL) & (near_y >= 0) & (near_y < CYL)
    first_pad = (local_x + 1) * (CYL + 2) + local_y + 1
    second_pad = (near_x + 1) * (CYL + 2) + near_y + 1

    def device_lists(dev_x, dev_y):
        glob_x = dev_x * CXL + local_x
        glob_y = dev_y * CYL + local_y
        other_x = glob_x + step_x
        other_y = glob_y + step_y
        in_grid = (other_x >= 0) & (other_x < NXC) & (other_y >= 0) & (other_y < NYC)
        base_x = jnp.clip(jnp.where(forward, glob_x, other_x), 0, NXC - 1)
        base_y = jnp.clip(jnp.where(forward, glob_y, other_y), 0, NYC - 1)
        is_alive = alive_table[base_x, base_y, direction] & in_grid
        owner_bit = roll_owner[base_x, base_y, direction]
        is_owned = in_block | jnp.where(forward, owner_bit == 0, owner_bit == 1)
        is_kept = is_alive & (forward | jnp.logical_not(in_block))
        category = jnp.where(is_kept, jnp.where(is_owned, 0, 1), 2).reshape(-1).astype(jnp.int32)
        ordering = jnp.argsort(category, stable=True)[:PAIR_SLOTS]
        pair_list = jnp.stack([first_pad.reshape(-1)[ordering], second_pad.reshape(-1)[ordering]])
        totals = jnp.stack([jnp.sum(category == 0), jnp.sum(category <= 1)]).astype(jnp.int32)
        return (pair_list.astype(jnp.int32), totals)
    grid_x, grid_y = jnp.meshgrid(jnp.arange(count_x, dtype=jnp.int32), jnp.arange(count_y, dtype=jnp.int32), indexing='ij')
    return jax.vmap(jax.vmap(device_lists))(grid_x, grid_y)


def draw_pair_cells(key, part):
    tables = pair_tables(key)
    return tables[0]


def draw_pair_counts(key, part):
    tables = pair_tables(key)
    return tables[1]


def draw_shell_nodes(key, part):
    key = jax.random.fold_in(key, 3)
    count_x = NXC // CXL
    local_ids = jax.random.randint(key, (MAPN, NXC, NYC), 0, NS_STRIP)
    local_ids = local_ids.at[2, NXC - 1, NYC - 1].set(NS_STRIP - 1)
    local_ids = local_ids.at[3, 0, 0].set(0)
    column_x = jnp.arange(NXC, dtype=jnp.int32)[None, :, None]
    strip_of = column_x // CXL
    inside_x = column_x % CXL
    slot_of = jnp.arange(MAPN, dtype=jnp.int32)[:, None, None]
    lower = (slot_of == 0) & (inside_x == 0) & (strip_of > 0)
    upper = (slot_of == 1) & (inside_x == CXL - 1) & (strip_of < count_x - 1)
    strips = jnp.where(lower, strip_of - 1, jnp.where(upper, strip_of + 1, strip_of))
    return (strips * NS_STRIP + local_ids).astype(jnp.int32)


def with_ends(drawn, stream_key, low, high):
    longest = drawn.shape.index(max(drawn.shape))
    spots = []
    for shift in (0, 1):
        where = [jax.random.randint(jax.random.fold_in(stream_key, axis), (), 0, length) for axis, length in enumerate(drawn.shape)]
        where[longest] = (where[longest] + shift) % drawn.shape[longest]
        spots.append(tuple(where))
    return drawn.at[spots[0]].set(low).at[spots[1]].set(high)


def levels(own_key, dims, cuts, low, high):
    factor_of, own = 1.0, jax.random.fold_in(own_key, 6)
    for axis_at, blocks in cuts:
        heights = jnp.exp(jax.random.uniform(jax.random.fold_in(own, axis_at), (blocks,), jnp.float32, low / len(cuts), high / len(cuts)))
        factor_of = factor_of * jnp.repeat(heights, dims[axis_at] // blocks).reshape([-1 if axis == axis_at else 1 for axis in range(len(dims))])
    return factor_of


def centred(stream_key, extent, width, most, shards=(), kind=jnp.bfloat16):
    result = width * jax.random.normal(stream_key, extent, jnp.float32)
    if shards:
        result = result * levels(stream_key, extent, shards, -0.22, 0.18)
    return jnp.clip(result, -most, most).astype(kind)


def setup_inputs(seed: int = 0) -> dict:
    splits = jax.random.split(jax.random.key(seed), 12)
    return {
        "positions": jnp.clip(1.0 * jax.random.uniform(splits[0], (3, NXC, NYC, CELL), jnp.float32) ** levels(splits[0], (3, NXC, NYC, CELL), ((1, 8), (2, 4)), -0.2, 0.2), 0.0, 1.0),
        "velocity": centred(splits[1], (3, NXC, NYC, CELL), 0.5, 3.0, ((1, 8), (2, 4)), jnp.float32),
        "density": jnp.clip(0.7 + 0.59999996 * jax.random.uniform(splits[2], (NXC, NYC, CELL), jnp.float32) ** levels(splits[2], (NXC, NYC, CELL), ((0, 8), (1, 4)), -0.2, 0.2), 0.7, 1.3),
        "cell_fill": with_ends(jax.random.randint(splits[3], (NXC, NYC), CELL // 4, CELL + 1), jax.random.fold_in(splits[3], 1), CELL // 4, CELL).astype(jnp.int32),
        "pair_cells": draw_pair_cells(jax.random.fold_in(splits[11], 71), 0),
        "pair_counts": draw_pair_counts(jax.random.fold_in(splits[11], 71), 0),
        "shell_nodes": draw_shell_nodes(jax.random.fold_in(splits[11], 71), 0),
        "shell_weights": jnp.clip(0.2 + 0.8 * jax.random.uniform(splits[7], (MAPN, NXC, NYC), jnp.float32) ** levels(splits[7], (MAPN, NXC, NYC), ((1, 8), (2, 4)), -0.2, 0.2), 0.2, 1.0),
        "shell_links": with_ends(jax.random.randint(splits[8], (LINKS, NS), 0, NS_STRIP), jax.random.fold_in(splits[8], 1), 0, NS_STRIP - 1).astype(jnp.int32),
        "shell_disp": centred(splits[9], (3, NS), 0.5, 3.0, ((1, 8),), jnp.float32),
        "shell_vel": centred(splits[10], (3, NS), 0.5, 3.0, ((1, 8),), jnp.float32),
    }


stiffness = 2.0
viscosity = 0.5
particle_mass = 0.02
time_step = 0.5
contact_depth = 0.5
wall_stiffness = 0.1
wall_drag = 0.2
shell_compliance = 0.2
shell_spring = 0.5
block_len = 16


def tile_fields(geo_a, geo_b, fluid_a, fluid_b, shift_x, shift_y):
    gap_x = (geo_a[0] + shift_x)[:, None] - geo_b[0][None, :]
    gap_y = (geo_a[1] + shift_y)[:, None] - geo_b[1][None, :]
    gap_z = geo_a[2][:, None] - geo_b[2][None, :]
    closeness = jnp.maximum(1.0 - (gap_x * gap_x + gap_y * gap_y + gap_z * gap_z), 0.0)
    weight = closeness * closeness * (geo_a[3][:, None] * geo_b[3][None, :])
    press_a = stiffness * (fluid_a[3] - 1.0)
    press_b = stiffness * (fluid_b[3] - 1.0)
    thrust = (press_a[:, None] + press_b[None, :]) * weight
    diff_x = fluid_a[0][:, None] - fluid_b[0][None, :]
    diff_y = fluid_a[1][:, None] - fluid_b[1][None, :]
    diff_z = fluid_a[2][:, None] - fluid_b[2][None, :]
    force_x = thrust * gap_x - viscosity * weight * diff_x
    force_y = thrust * gap_y - viscosity * weight * diff_y
    force_z = thrust * gap_z - viscosity * weight * diff_z
    density_rate = weight * (diff_x * gap_x + diff_y * gap_y + diff_z * gap_z)
    return force_x, force_y, force_z, density_rate


def self_terms(geo_a, fluid_a):
    fields = tile_fields(geo_a, geo_a, fluid_a, fluid_a, 0.0, 0.0)
    return jnp.stack([jnp.sum(fields[0], 1), jnp.sum(fields[1], 1), jnp.sum(fields[2], 1), jnp.sum(fields[3], 1)])


def pair_terms(geo_a, geo_b, fluid_a, fluid_b, shift_x, shift_y):
    fields = tile_fields(geo_a, geo_b, fluid_a, fluid_b, shift_x, shift_y)
    row_sums = jnp.stack([jnp.sum(fields[0], 1), jnp.sum(fields[1], 1), jnp.sum(fields[2], 1), jnp.sum(fields[3], 1)])
    col_sums = jnp.stack([-jnp.sum(fields[0], 0), -jnp.sum(fields[1], 0), -jnp.sum(fields[2], 0), jnp.sum(fields[3], 0)])
    return row_sums, col_sums


def wall_force(positions, velocity, live_mask, coupled):
    contact = jnp.maximum(1.0 - positions[2] / contact_depth, 0.0)
    contact = contact * contact * live_mask
    drag = wall_drag * contact * (coupled[..., None] - velocity)
    return drag.at[2].add(wall_stiffness * contact)


def shell_update(disp, shell_speed, node_force, links):
    beside_all = jnp.sum(disp[:, links], 1)
    spring_force = links.shape[0] * disp - beside_all
    new_speed = shell_speed + time_step * (shell_compliance * node_force - shell_spring * spring_force)
    return new_speed, disp + time_step * new_speed


def pad_blocks(values, filler):
    extra = (-values.shape[0]) % block_len
    padded = jnp.concatenate([values, jnp.full((extra,), filler, values.dtype)])
    return padded.reshape(-1, block_len)


def reference(positions, velocity, density, cell_fill, pair_cells, pair_counts, shell_nodes, shell_weights, shell_links, shell_disp, shell_vel):
    ny_pad = CYL + 2
    ncell = NXC * NYC
    slot_iota = lax.broadcasted_iota(jnp.int32, (NXC, NYC, CELL), 2)
    live_mask = (slot_iota < cell_fill[:, :, None]).astype(jnp.float32)
    geometry = jnp.concatenate([positions, live_mask[None]], 0).reshape(4, ncell, CELL)
    dev_x = (jnp.arange(N_GX, dtype=jnp.int32) * CXL)[:, None, None]
    dev_y = (jnp.arange(N_GY, dtype=jnp.int32) * CYL)[None, :, None]
    first_x = dev_x + pair_cells[:, :, 0, :] // ny_pad - 1
    first_y = dev_y + pair_cells[:, :, 0, :] % ny_pad - 1
    second_x = dev_x + pair_cells[:, :, 1, :] // ny_pad - 1
    second_y = dev_y + pair_cells[:, :, 1, :] % ny_pad - 1
    pair_iota = jnp.arange(PAIR_SLOTS, dtype=jnp.int32)[None, None, :]
    is_live = pad_blocks((pair_iota < pair_counts[:, :, 0:1]).astype(jnp.float32).reshape(-1), 0.0)
    shift_x = pad_blocks((first_x - second_x).astype(jnp.float32).reshape(-1), 0.0)
    shift_y = pad_blocks((first_y - second_y).astype(jnp.float32).reshape(-1), 0.0)
    first = pad_blocks((jnp.clip(first_x, 0, NXC - 1) * NYC + jnp.clip(first_y, 0, NYC - 1)).reshape(-1).astype(jnp.int32), 0)
    second = pad_blocks((jnp.clip(second_x, 0, NXC - 1) * NYC + jnp.clip(second_y, 0, NYC - 1)).reshape(-1).astype(jnp.int32), 0)
    cell_ids = jnp.arange(ncell, dtype=jnp.int32).reshape(-1, block_len)
    strip_base = (jnp.arange(NS, dtype=jnp.int32) // NS_STRIP) * NS_STRIP
    links = shell_links + strip_base[None, :]
    for substep in range(SUBSTEPS):
        fluid = jnp.concatenate([velocity, density[None]], 0).reshape(4, ncell, CELL)

        def self_step(sums, picked):
            row_sums = jax.vmap(self_terms, in_axes=(1, 1), out_axes=1)(geometry[:, picked], fluid[:, picked])
            return sums.at[:, picked].add(row_sums), None

        sums, unused = lax.scan(self_step, jnp.zeros((4, ncell, CELL), jnp.float32), cell_ids)

        def pair_step(sums, block):
            first_b, second_b, sx_b, sy_b, live_b = block
            row_sums, col_sums = jax.vmap(pair_terms, in_axes=(1, 1, 1, 1, 0, 0), out_axes=1)(
                geometry[:, first_b], geometry[:, second_b], fluid[:, first_b], fluid[:, second_b], sx_b, sy_b)
            sums = sums.at[:, first_b].add(row_sums * live_b[None, :, None])
            return sums.at[:, second_b].add(col_sums * live_b[None, :, None]), None

        sums, unused = lax.scan(pair_step, sums, (first, second, shift_x, shift_y, is_live))
        forces = sums.reshape(4, NXC, NYC, CELL)
        coupled = jnp.sum(shell_vel[:, shell_nodes] * shell_weights[None], 1)
        wall_push = wall_force(positions, velocity, live_mask, coupled)
        wall_load = -jnp.sum(wall_push, 3)
        shares = shell_weights[None] * wall_load[:, None]
        node_force = jnp.zeros((3, NS), jnp.float32).at[:, shell_nodes].add(shares)
        shell_vel, shell_disp = shell_update(shell_disp, shell_vel, node_force, links)
        velocity = velocity + time_step * (particle_mass * forces[0:3] + wall_push)
        density = density + time_step * particle_mass * forces[3]
    return velocity, density, shell_vel, shell_disp
```

```python
import functools

import jax
import jax.numpy as jnp
from jax import lax
from jax.experimental import pallas as pl
from jax.experimental.pallas import tpu as pltpu
from jax.sharding import PartitionSpec as P

F32 = jnp.float32
BF16 = jnp.bfloat16
MESH = pl.DeviceIdType.MESH
LANES = 128
DIRS = [(a, b) for a in (-1, 0, 1) for b in (-1, 0, 1)]


def iota(shape, dim):
    return lax.broadcasted_iota(jnp.int32, shape, dim)


def split3(value):
    high = value.astype(BF16).astype(F32)
    rest = value - high
    mid = rest.astype(BF16).astype(F32)
    low = (rest - mid).astype(BF16).astype(F32)
    return high, mid, low


def dot(a, b):
    return jnp.dot(a, b, preferred_element_type=F32)


def dot_t(a, b):
    return lax.dot_general(a, b, (((1,), (1,)), ((), ())), preferred_element_type=F32)


def table_of(rows):
    return jnp.concatenate(split3(rows), axis=1).astype(BF16)


def kernel(
    nx, ny,
    pos_ref, vel_ref, rho_ref, fill_ref, pairs_ref, counts_ref, ties_ref, links_ref, disp_ref, svel_ref,
    vel_out, rho_out, speed_out, offset_out,
    posS, velS, rhoS, liveS, pushS, forS, pad1, pad2, win1, win2, msg1, msg2,
    alive, dtab, dtable, beside, node, left, right, loads, whigh, wlow,
    halo_send, halo_recv, win_send, win_recv, msg_send, msg_recv,
):
    cxl, cyl, cell = rho_ref.shape
    cells = cxl * cyl
    nyp = cyl + 2
    nodes = svel_ref.shape[1]
    nhi = nodes // LANES
    ties = 4 * cells
    x, y = lax.axis_index("gx"), lax.axis_index("gy")

    def peer(a, b):
        return (lax.rem(x + a + nx, nx), lax.rem(y + b + ny, ny))

    def slot_of(a, b):
        return (a + 1) * ny + lax.rem(y + b + ny, ny)

    peers = [(a, b) for a in (-1, 0, 1) for b in range(ny) if (a, b) != (0, 0)]
    barrier = pltpu.get_barrier_semaphore()
    for a, b in peers:
        pl.semaphore_signal(barrier, inc=1, device_id=peer(a, b), device_id_type=MESH)

    lane_cell = iota((1, cell), 1)
    for i in range(cxl):
        rows = pl.ds(i * cyl, cyl)
        for c in range(3):
            posS[c, rows, :] = pos_ref[c, i]
            velS[c, rows, :] = vel_ref[c, i]
        rhoS[rows, :] = rho_ref[i]
        for j in range(cyl):
            liveS[pl.ds(i * cyl + j, 1), :] = jnp.where(lane_cell < fill_ref[i, j], 1.0, 0.0).astype(F32)

    def fill_pad(pad):
        def row(i, carry):
            for j in range(cyl):
                one = pl.ds(i * cyl + j, 1)
                for c in range(3):
                    pad[i + 1, j + 1, c : c + 1, :] = posS[c, one, :]
                    pad[i + 1, j + 1, 4 + c : 5 + c, :] = velS[c, one, :]
                pad[i + 1, j + 1, 3:4, :] = liveS[one, :]
                pad[i + 1, j + 1, 7:8, :] = rhoS[one, :]
            return carry

        lax.fori_loop(0, cxl, row, 0)

    def to_rows(source, target, index):
        def step(h, carry):
            at = pl.ds(pl.multiple_of(h * LANES, LANES), LANES)
            for c in range(3):
                if index is None:
                    target[pl.ds(c * nhi + h, 1), :] = source[c : c + 1, at]
                else:
                    target[index, pl.ds(c * nhi + h, 1), :] = source[c : c + 1, at]
            return carry

        lax.fori_loop(0, nhi, step, 0)

    def halo_copies(pad, at):
        def cut(d, size):
            if d == 0:
                return pl.ds(1, size), pl.ds(1, size)
            return (pl.ds(size, 1), pl.ds(0, 1)) if d > 0 else (pl.ds(1, 1), pl.ds(size + 1, 1))

        out = []
        for k, (a, b) in enumerate([d for d in DIRS if d != (0, 0)]):
            (sx, tx), (sy, ty) = cut(a, cxl), cut(b, cyl)
            out.append(
                pltpu.make_async_remote_copy(
                    src_ref=pad.at[sx, sy], dst_ref=pad.at[tx, ty],
                    send_sem=halo_send.at[at, k], recv_sem=halo_recv.at[at, k],
                    device_id=peer(a, b), device_id_type=MESH,
                )
            )
        return out

    def win_copies(win, at):
        return [
            pltpu.make_async_remote_copy(
                src_ref=win.at[1], dst_ref=win.at[1 - a],
                send_sem=win_send.at[at, k], recv_sem=win_recv.at[at, k],
                device_id=peer(a, 0), device_id_type=MESH,
            )
            for k, a in enumerate((-1, 1))
        ]

    def msg_copy(msg, at, k, a, b, slot):
        return pltpu.make_async_remote_copy(
            src_ref=msg.at[ny + y], dst_ref=msg.at[slot],
            send_sem=msg_send.at[at, k], recv_sem=msg_recv.at[at, slot],
            device_id=peer(a, b), device_id_type=MESH,
        )

    fill_pad(pad1)
    to_rows(svel_ref, win1, 1)
    pl.semaphore_wait(barrier, len(peers))
    wins = win_copies(win1, 0)
    for copy in wins:
        copy.start()
    halos = halo_copies(pad1, 0)
    for copy in halos:
        copy.start()

    slots = pairs_ref.shape[1]
    own = iota((cells, slots), 0)
    here = (own // cyl + 1) * nyp + own % cyl + 1
    listed = iota((cells, slots), 1) < counts_ref[0, 1]
    first, second = pairs_ref[0:1, :], pairs_ref[1:2, :]
    for k, (a, b) in enumerate(DIRS):
        if (a, b) == (0, 0):
            alive[k] = jnp.ones((cells, cell), F32)
            continue
        there = here + a * nyp + b
        found = ((first == here) & (second == there)) | ((first == there) & (second == here))
        count = jnp.sum(jnp.where(found & listed, 1.0, 0.0).astype(F32), axis=1, keepdims=True)
        alive[k] = jnp.broadcast_to(count, (cells, cell))

    block = 512

    def springs(disp):
        to_rows(disp, dtab, None)
        dtable[...] = table_of(dtab[...])

        def step(j, carry):
            at = pl.ds(pl.multiple_of(j * block, block), block)
            sums = [jnp.zeros((nhi, block), F32) for c in range(3)]
            for l in range(links_ref.shape[0]):
                index = links_ref[l : l + 1, at]
                low, high = index & (LANES - 1), index >> 7
                hot = jnp.where(iota((LANES, block), 0) == low, 1.0, 0.0).astype(BF16)
                got = dot(dtable[...], jnp.concatenate([hot, hot, hot], axis=0))
                at_high = iota((nhi, block), 0) == high
                for c in range(3):
                    sums[c] = sums[c] + jnp.where(at_high, got[c * nhi : (c + 1) * nhi], 0.0)
            for c in range(3):
                beside[c : c + 1, at] = jnp.sum(sums[c], axis=0, keepdims=True)
            return carry

        lax.fori_loop(0, nodes // block, step, 0)

    id_row, weight_row = ties_ref[0:1, :], ties_ref[1:2, :]
    diag = iota((ties, LANES), 0) == iota((ties, LANES), 1)
    id_col = jnp.sum(jnp.where(diag, id_row, 0.0), axis=1, keepdims=True)
    weight_col = jnp.sum(jnp.where(diag, weight_row, 0.0), axis=1, keepdims=True)

    def wall(win, msg, at):
        place = id_col.astype(jnp.int32) - (x - 1) * nodes
        low, high = place & (LANES - 1), place >> 7
        hot = jnp.where(iota((ties, LANES), 1) == low, 1.0, 0.0).astype(BF16)
        hot = jnp.concatenate([hot, hot, hot], axis=1)
        value = [jnp.zeros((ties, 1), F32) for c in range(3)]
        lane = iota((ties, 3 * nhi), 1)
        for strip in range(3):
            got = dot_t(hot, table_of(win[strip]))
            inside = high - strip * nhi
            fits = (inside >= 0) & (inside < nhi)
            for c in range(3):
                pick = fits & (lane == inside + c * nhi)
                value[c] = value[c] + jnp.sum(jnp.where(pick, got, 0.0), axis=1, keepdims=True)
        contact = jnp.maximum(1.0 - 2.0 * posS[2], 0.0)
        contact = contact * contact * liveS[...]
        mine = ny + y
        msg[mine] = jnp.zeros((8, LANES), F32)
        spread = iota((cells, LANES), 0) == (iota((cells, LANES), 1) & (cells - 1))
        for c in range(3):
            tied = value[c] * weight_col
            coupled = sum(tied[k * cells : (k + 1) * cells] for k in range(4))
            push = 0.2 * contact * (coupled - velS[c])
            if c == 2:
                push = push + 0.1 * contact
            pushS[c] = push
            load = -jnp.sum(push, axis=1, keepdims=True)
            row = jnp.sum(jnp.where(spread, load, 0.0), axis=0, keepdims=True)
            msg[mine, c : c + 1, :] = row * weight_row
        msg[mine, 3:4, :] = id_row
        for k, (a, b) in enumerate(peers):
            msg_copy(msg, at, k, a, b, (1 - a) * ny + y).start()

    def shell_step(msg, at, speed, disp):
        for k, (a, b) in enumerate(peers):
            msg_copy(msg, at, k, a, b, slot_of(a, b)).wait_recv()

        def add(s, total):
            note = msg[s]
            place = note[3:4].astype(jnp.int32) - x * nodes
            low, high = place & (LANES - 1), place >> 7
            at_high = iota((nhi, LANES), 0) == high
            share = jnp.concatenate([jnp.where(at_high, note[c : c + 1], 0.0) for c in range(3)], axis=0)
            hot = jnp.where(iota((LANES, LANES), 0) == low, 1.0, 0.0).astype(BF16)
            return total + dot_t(table_of(share), jnp.concatenate([hot, hot, hot], axis=1))

        dtab[...] = lax.fori_loop(0, 3 * ny, add, jnp.zeros((3 * nhi, LANES), F32))

        def row(h, carry):
            for c in range(3):
                node[c : c + 1, pl.ds(pl.multiple_of(h * LANES, LANES), LANES)] = dtab[pl.ds(c * nhi + h, 1), :]
            return carry

        lax.fori_loop(0, nhi, row, 0)
        old = disp[...]
        spring = 4.0 * old - beside[...]
        new = speed[...] + 0.5 * (0.2 * node[...] - 0.5 * spring)
        speed_out[...] = new
        offset_out[...] = old + 0.5 * new

    row8 = iota((8, cell), 0)

    def geometry(pad, i, j):
        field = pad[i, j]
        shift_x = (i - 3).astype(F32) if not isinstance(i, int) else float(i - 3)
        shift_y = (j - 3).astype(F32) if not isinstance(j, int) else float(j - 3)
        shift = jnp.where(row8 == 0, shift_x, jnp.where(row8 == 1, shift_y, -0.5))
        xyz = jnp.where(row8 < 3, field + shift, 0.0)
        return field, xyz

    def along(field, xyz):
        return xyz[0:1] * field[4:5] + xyz[1:2] * field[5:6] + xyz[2:3] * field[6:7]

    def geo_tables(pad):
        def step(p, carry):
            field, xyz = geometry(pad, p // nyp, p % nyp)
            square = jnp.sum(xyz * xyz, axis=0, keepdims=True)
            to = jnp.where(row8 < 3, xyz, jnp.where(row8 == 3, 1.0 - square, jnp.where(row8 == 4, -1.0, 0.0)))
            by = jnp.where(row8 < 3, 2.0 * xyz, jnp.where(row8 == 3, 1.0, jnp.where(row8 == 4, square, 0.0)))
            th, tm, tl = split3(to)
            bh, bm, bl = split3(by)
            right[p] = jnp.concatenate([th, tm, th, tm, tl, th], axis=0).astype(BF16)
            turned = jnp.concatenate([bh, bh, bm, bm, bh, bl] + [jnp.zeros((8, cell), F32)] * 10, axis=0)
            left[p] = jnp.transpose(turned)[:, :48].astype(BF16)
            return carry

        lax.fori_loop(0, (cxl + 2) * nyp, step, 0)

    def load_tables(pad):
        def step(p, carry):
            field, xyz = geometry(pad, p // nyp, p % nyp)
            live, press = field[3:4], 2.0 * (field[7:8] - 1.0)
            flat = jnp.where(row8 < 3, xyz, jnp.where(row8 == 3, 1.0, jnp.where(row8 == 7, along(field, xyz), field)))
            flat = flat * live
            pressed = jnp.where(row8 < 4, flat, 0.0) * press
            fh, fm, fl = split3(flat)
            ph, pm, pm2 = split3(pressed)
            loads[p] = jnp.concatenate([fh, ph, fm, pm, fl, pm2], axis=0).astype(BF16)
            return carry

        lax.fori_loop(0, (cxl + 2) * nyp, step, 0)

    chunk = 64

    def forces(pad, fresh):
        def step(own_cell, carry):
            i, j = own_cell // cyl + 1, own_cell % cyl + 1
            here = i * nyp + j
            total = jnp.zeros((48, cell), F32)
            for k, (a, b) in enumerate(DIRS):
                there = here + a * nyp + b
                tile = own_cell * 9 + k
                if fresh:
                    for s in range(cell // chunk):
                        part = pl.ds(s * chunk, chunk)
                        close = jnp.maximum(dot(left[there, part, :], right[here]), 0.0)
                        weight = close * close
                        high = weight.astype(BF16)
                        whigh[tile, part, :] = high
                        wlow[tile, part, :] = (weight - high.astype(F32)).astype(BF16)
                summed = dot(loads[there], whigh[tile]) + dot(loads[there], wlow[tile])
                total = total + summed * alive[k, pl.ds(own_cell, 1), :]
            total = total[0:16] + total[16:32] + total[32:48]
            field, xyz = geometry(pad, i, j)
            live, press = field[3:4], 2.0 * (field[7:8] - 1.0)
            count, pressure = total[3:4], total[11:12]
            rate = along(field, xyz) * count + total[7:8]
            for c in range(3):
                at, speed = xyz[c : c + 1], field[4 + c : 5 + c]
                moved, sped = total[c : c + 1], total[4 + c : 5 + c]
                push = press * (at * count - moved) + at * pressure - total[8 + c : 9 + c]
                push = push - 0.5 * (speed * count - sped)
                forS[c, pl.ds(own_cell, 1), :] = push * live
                rate = rate - speed * moved - at * sped
            forS[3, pl.ds(own_cell, 1), :] = rate * live
            return carry

        lax.fori_loop(0, cells, step, 0)

    def advance():
        for c in range(3):
            velS[c] = velS[c] + 0.5 * (0.02 * forS[c] + pushS[c])
        rhoS[...] = rhoS[...] + 0.5 * 0.02 * forS[3]

    springs(disp_ref)
    for copy in wins:
        copy.wait_recv()
    wall(win1, msg1, 0)
    for copy in halos:
        copy.wait_recv()
    geo_tables(pad1)
    load_tables(pad1)
    forces(pad1, True)
    advance()
    fill_pad(pad2)
    halos2 = halo_copies(pad2, 1)
    for copy in halos2:
        copy.start()
    shell_step(msg1, 0, svel_ref, disp_ref)
    to_rows(speed_out, win2, 1)
    wins2 = win_copies(win2, 1)
    for copy in wins2:
        copy.start()
    springs(offset_out)
    for copy in wins2:
        copy.wait_recv()
    wall(win2, msg2, 1)
    for copy in halos2:
        copy.wait_recv()
    load_tables(pad2)
    forces(pad2, False)
    advance()
    for i in range(cxl):
        rows = pl.ds(i * cyl, cyl)
        for c in range(3):
            vel_out[c, i] = velS[c, rows, :]
        rho_out[i] = rhoS[rows, :]
    shell_step(msg2, 1, speed_out, offset_out)
    for copy in wins + halos + wins2 + halos2:
        copy.wait_send()
    for at, msg in enumerate((msg1, msg2)):
        for k, (a, b) in enumerate(peers):
            msg_copy(msg, at, k, a, b, slot_of(a, b)).wait_send()


def body(nx, ny, positions, velocity, density, cell_fill, pair_cells, pair_counts,
         shell_nodes, shell_weights, shell_links, shell_disp, shell_vel):
    cxl, cyl, cell = density.shape
    cells, pads = cxl * cyl, (cxl + 2) * (cyl + 2)
    nodes = shell_vel.shape[1]
    nhi = nodes // LANES
    entries = shell_nodes.size
    ties = jnp.stack([shell_nodes.reshape(-1).astype(F32), shell_weights.reshape(-1)])
    ties = jnp.pad(ties, ((0, 6), (0, LANES - entries)))
    npeers = 3 * ny
    vmem = pl.BlockSpec(memory_space=pltpu.VMEM)
    smem = pl.BlockSpec(memory_space=pltpu.SMEM)
    return pl.pallas_call(
        functools.partial(kernel, nx, ny),
        out_shape=[
            jax.ShapeDtypeStruct(velocity.shape, F32),
            jax.ShapeDtypeStruct(density.shape, F32),
            jax.ShapeDtypeStruct(shell_vel.shape, F32),
            jax.ShapeDtypeStruct(shell_disp.shape, F32),
        ],
        in_specs=[vmem, vmem, vmem, smem, vmem, smem, vmem, vmem, vmem, vmem],
        out_specs=[vmem] * 4,
        scratch_shapes=[
            pltpu.VMEM((3, cells, cell), F32),
            pltpu.VMEM((3, cells, cell), F32),
            pltpu.VMEM((cells, cell), F32),
            pltpu.VMEM((cells, cell), F32),
            pltpu.VMEM((3, cells, cell), F32),
            pltpu.VMEM((4, cells, cell), F32),
            pltpu.VMEM((cxl + 2, cyl + 2, 8, cell), F32),
            pltpu.VMEM((cxl + 2, cyl + 2, 8, cell), F32),
            pltpu.VMEM((3, 3 * nhi, LANES), F32),
            pltpu.VMEM((3, 3 * nhi, LANES), F32),
            pltpu.VMEM((npeers, 8, LANES), F32),
            pltpu.VMEM((npeers, 8, LANES), F32),
            pltpu.VMEM((9, cells, cell), F32),
            pltpu.VMEM((3 * nhi, LANES), F32),
            pltpu.VMEM((3 * nhi, 3 * LANES), BF16),
            pltpu.VMEM((3, nodes), F32),
            pltpu.VMEM((3, nodes), F32),
            pltpu.VMEM((pads, cell, 48), BF16),
            pltpu.VMEM((pads, 48, cell), BF16),
            pltpu.VMEM((pads, 48, cell), BF16),
            pltpu.VMEM((cells * 9, cell, cell), BF16),
            pltpu.VMEM((cells * 9, cell, cell), BF16),
            pltpu.SemaphoreType.DMA((2, 8)),
            pltpu.SemaphoreType.DMA((2, 8)),
            pltpu.SemaphoreType.DMA((2, 2)),
            pltpu.SemaphoreType.DMA((2, 2)),
            pltpu.SemaphoreType.DMA((2, npeers)),
            pltpu.SemaphoreType.DMA((2, npeers)),
        ],
        compiler_params=pltpu.CompilerParams(
            collective_id=0, has_side_effects=True, vmem_limit_bytes=56 * 1024 * 1024
        ),
        name="hydro",
    )(positions, velocity, density, cell_fill, pair_cells[0, 0], pair_counts[0], ties,
      shell_links, shell_disp, shell_vel)


def solution(mesh):
    nx, ny = mesh.shape["gx"], mesh.shape["gy"]
    return jax.shard_map(
        functools.partial(body, nx, ny),
        mesh=mesh,
        in_specs=(
            P(None, "gx", "gy", None),
            P(None, "gx", "gy", None),
            P("gx", "gy", None),
            P("gx", "gy"),
            P("gx", "gy", None, None),
            P("gx", "gy", None),
            P(None, "gx", "gy"),
            P(None, "gx", "gy"),
            P(None, "gx"),
            P(None, "gx"),
            P(None, "gx"),
        ),
        out_specs=(P(None, "gx", "gy", None), P("gx", "gy", None), P(None, "gx"), P(None, "gx")),
        check_vma=False,
    )
```

```python
import functools

import jax
import jax.numpy as jnp
from jax import lax
from jax.experimental import pallas as pl
from jax.experimental.pallas import tpu as pltpu
from jax.sharding import PartitionSpec as P

F32 = jnp.float32
BF16 = jnp.bfloat16
MESH = pl.DeviceIdType.MESH
LANES = 128
DIRS = [(a, b) for a in (-1, 0, 1) for b in (-1, 0, 1)]


def iota(shape, dim):
    return lax.broadcasted_iota(jnp.int32, shape, dim)


def split3(value):
    high = value.astype(BF16).astype(F32)
    rest = value - high
    mid = rest.astype(BF16).astype(F32)
    low = (rest - mid).astype(BF16).astype(F32)
    return high, mid, low


def dot(a, b):
    return jnp.dot(a, b, preferred_element_type=F32)


def dot_t(a, b):
    return lax.dot_general(a, b, (((1,), (1,)), ((), ())), preferred_element_type=F32)


def table_of(rows):
    return jnp.concatenate(split3(rows), axis=1).astype(BF16)


def kernel(
    nx, ny,
    pos_ref, vel_ref, rho_ref, fill_ref, pairs_ref, counts_ref, ties_ref, links_ref, disp_ref, svel_ref,
    vel_out, rho_out, speed_out, offset_out,
    posS, velS, rhoS, liveS, pushS, forS, pad1, pad2, win1, win2, msg1, msg2,
    alive, dtab, dtable, beside, node, left, right, loads, whigh, wlow, totals,
    halo_send, halo_recv, win_send, win_recv, msg_send, msg_recv,
):
    cxl, cyl, cell = rho_ref.shape
    cells = cxl * cyl
    nyp = cyl + 2
    nodes = svel_ref.shape[1]
    nhi = nodes // LANES
    ties = 4 * cells
    x, y = lax.axis_index("gx"), lax.axis_index("gy")

    def peer(a, b):
        return (lax.rem(x + a + nx, nx), lax.rem(y + b + ny, ny))

    def slot_of(a, b):
        return (a + 1) * ny + lax.rem(y + b + ny, ny)

    peers = [(a, b) for a in (-1, 0, 1) for b in range(ny) if (a, b) != (0, 0)]
    barrier = pltpu.get_barrier_semaphore()
    for a, b in peers:
        pl.semaphore_signal(barrier, inc=1, device_id=peer(a, b), device_id_type=MESH)

    lane_cell = iota((1, cell), 1)
    for i in range(cxl):
        rows = pl.ds(i * cyl, cyl)
        for c in range(3):
            posS[c, rows, :] = pos_ref[c, i]
            velS[c, rows, :] = vel_ref[c, i]
        rhoS[rows, :] = rho_ref[i]
        for j in range(cyl):
            liveS[pl.ds(i * cyl + j, 1), :] = jnp.where(lane_cell < fill_ref[i, j], 1.0, 0.0).astype(F32)

    def fill_pad(pad):
        def row(i, carry):
            for j in range(cyl):
                one = pl.ds(i * cyl + j, 1)
                for c in range(3):
                    pad[i + 1, j + 1, c : c + 1, :] = posS[c, one, :]
                    pad[i + 1, j + 1, 4 + c : 5 + c, :] = velS[c, one, :]
                pad[i + 1, j + 1, 3:4, :] = liveS[one, :]
                pad[i + 1, j + 1, 7:8, :] = rhoS[one, :]
            return carry

        lax.fori_loop(0, cxl, row, 0, unroll=True)

    def to_rows(source, target, index):
        def step(h, carry):
            at = pl.ds(pl.multiple_of(h * LANES, LANES), LANES)
            for c in range(3):
                if index is None:
                    target[pl.ds(c * nhi + h, 1), :] = source[c : c + 1, at]
                else:
                    target[index, pl.ds(c * nhi + h, 1), :] = source[c : c + 1, at]
            return carry

        lax.fori_loop(0, nhi, step, 0, unroll=8)

    def halo_copies(pad, at):
        def cut(d, size):
            if d == 0:
                return pl.ds(1, size), pl.ds(1, size)
            return (pl.ds(size, 1), pl.ds(0, 1)) if d > 0 else (pl.ds(1, 1), pl.ds(size + 1, 1))

        out = []
        for k, (a, b) in enumerate([d for d in DIRS if d != (0, 0)]):
            (sx, tx), (sy, ty) = cut(a, cxl), cut(b, cyl)
            out.append(
                pltpu.make_async_remote_copy(
                    src_ref=pad.at[sx, sy], dst_ref=pad.at[tx, ty],
                    send_sem=halo_send.at[at, k], recv_sem=halo_recv.at[at, k],
                    device_id=peer(a, b), device_id_type=MESH,
                )
            )
        return out

    def win_copies(win, at):
        return [
            pltpu.make_async_remote_copy(
                src_ref=win.at[1], dst_ref=win.at[1 - a],
                send_sem=win_send.at[at, k], recv_sem=win_recv.at[at, k],
                device_id=peer(a, 0), device_id_type=MESH,
            )
            for k, a in enumerate((-1, 1))
        ]

    def msg_copy(msg, at, k, a, b, slot):
        return pltpu.make_async_remote_copy(
            src_ref=msg.at[ny + y], dst_ref=msg.at[slot],
            send_sem=msg_send.at[at, k], recv_sem=msg_recv.at[at, slot],
            device_id=peer(a, b), device_id_type=MESH,
        )

    fill_pad(pad1)
    to_rows(svel_ref, win1, 1)
    pl.semaphore_wait(barrier, len(peers))
    wins = win_copies(win1, 0)
    for copy in wins:
        copy.start()
    halos = halo_copies(pad1, 0)
    for copy in halos:
        copy.start()

    slots = pairs_ref.shape[1]
    own = iota((cells, slots), 0)
    here = (own // cyl + 1) * nyp + own % cyl + 1
    listed = iota((cells, slots), 1) < counts_ref[0, 1]
    first, second = pairs_ref[0:1, :], pairs_ref[1:2, :]
    for k, (a, b) in enumerate(DIRS):
        if (a, b) == (0, 0):
            alive[k] = jnp.ones((cells, cell), F32)
            continue
        there = here + a * nyp + b
        found = ((first == here) & (second == there)) | ((first == there) & (second == here))
        count = jnp.sum(jnp.where(found & listed, 1.0, 0.0).astype(F32), axis=1, keepdims=True)
        alive[k] = jnp.broadcast_to(count, (cells, cell))

    block = 512

    def springs(disp):
        to_rows(disp, dtab, None)
        dtable[...] = table_of(dtab[...])

        def step(j, carry):
            at = pl.ds(pl.multiple_of(j * block, block), block)
            sums = [jnp.zeros((nhi, block), F32) for c in range(3)]
            for l in range(links_ref.shape[0]):
                index = links_ref[l : l + 1, at]
                low, high = index & (LANES - 1), index >> 7
                hot = jnp.where(iota((LANES, block), 0) == low, 1.0, 0.0).astype(BF16)
                got = dot(dtable[...], jnp.concatenate([hot, hot, hot], axis=0))
                at_high = iota((nhi, block), 0) == high
                for c in range(3):
                    sums[c] = sums[c] + jnp.where(at_high, got[c * nhi : (c + 1) * nhi], 0.0)
            for c in range(3):
                beside[c : c + 1, at] = jnp.sum(sums[c], axis=0, keepdims=True)
            return carry

        lax.fori_loop(0, nodes // block, step, 0)

    id_row, weight_row = ties_ref[0:1, :], ties_ref[1:2, :]
    diag = iota((ties, LANES), 0) == iota((ties, LANES), 1)
    id_col = jnp.sum(jnp.where(diag, id_row, 0.0), axis=1, keepdims=True)
    weight_col = jnp.sum(jnp.where(diag, weight_row, 0.0), axis=1, keepdims=True)

    def wall(win, msg, at):
        place = id_col.astype(jnp.int32) - (x - 1) * nodes
        low, high = place & (LANES - 1), place >> 7
        hot = jnp.where(iota((ties, LANES), 1) == low, 1.0, 0.0).astype(BF16)
        hot = jnp.concatenate([hot, hot, hot], axis=1)
        value = [jnp.zeros((ties, 1), F32) for c in range(3)]
        lane = iota((ties, 3 * nhi), 1)
        for strip in range(3):
            got = dot_t(hot, table_of(win[strip]))
            inside = high - strip * nhi
            fits = (inside >= 0) & (inside < nhi)
            for c in range(3):
                pick = fits & (lane == inside + c * nhi)
                value[c] = value[c] + jnp.sum(jnp.where(pick, got, 0.0), axis=1, keepdims=True)
        contact = jnp.maximum(1.0 - 2.0 * posS[2], 0.0)
        contact = contact * contact * liveS[...]
        mine = ny + y
        msg[mine] = jnp.zeros((8, LANES), F32)
        spread = iota((cells, LANES), 0) == (iota((cells, LANES), 1) & (cells - 1))
        for c in range(3):
            tied = value[c] * weight_col
            coupled = sum(tied[k * cells : (k + 1) * cells] for k in range(4))
            push = 0.2 * contact * (coupled - velS[c])
            if c == 2:
                push = push + 0.1 * contact
            pushS[c] = push
            load = -jnp.sum(push, axis=1, keepdims=True)
            row = jnp.sum(jnp.where(spread, load, 0.0), axis=0, keepdims=True)
            msg[mine, c : c + 1, :] = row * weight_row
        msg[mine, 3:4, :] = id_row
        for k, (a, b) in enumerate(peers):
            msg_copy(msg, at, k, a, b, (1 - a) * ny + y).start()

    def shell_step(msg, at, speed, disp):
        for k, (a, b) in enumerate(peers):
            msg_copy(msg, at, k, a, b, slot_of(a, b)).wait_recv()

        def add(s, total):
            note = msg[s]
            place = note[3:4].astype(jnp.int32) - x * nodes
            low, high = place & (LANES - 1), place >> 7
            at_high = iota((nhi, LANES), 0) == high
            share = jnp.concatenate([jnp.where(at_high, note[c : c + 1], 0.0) for c in range(3)], axis=0)
            hot = jnp.where(iota((LANES, LANES), 0) == low, 1.0, 0.0).astype(BF16)
            return total + dot_t(table_of(share), jnp.concatenate([hot, hot, hot], axis=1))

        dtab[...] = lax.fori_loop(0, 3 * ny, add, jnp.zeros((3 * nhi, LANES), F32), unroll=6)

        def row(h, carry):
            for c in range(3):
                node[c : c + 1, pl.ds(pl.multiple_of(h * LANES, LANES), LANES)] = dtab[pl.ds(c * nhi + h, 1), :]
            return carry

        lax.fori_loop(0, nhi, row, 0, unroll=8)
        old = disp[...]
        spring = 4.0 * old - beside[...]
        new = speed[...] + 0.5 * (0.2 * node[...] - 0.5 * spring)
        speed_out[...] = new
        offset_out[...] = old + 0.5 * new

    row8 = iota((8, cell), 0)

    def geometry(pad, i, j):
        field = pad[i, j]
        shift_x = (i - 3).astype(F32) if not isinstance(i, int) else float(i - 3)
        shift_y = (j - 3).astype(F32) if not isinstance(j, int) else float(j - 3)
        shift = jnp.where(row8 == 0, shift_x, jnp.where(row8 == 1, shift_y, -0.5))
        xyz = jnp.where(row8 < 3, field + shift, 0.0)
        return field, xyz

    def along(field, xyz):
        return xyz[0:1] * field[4:5] + xyz[1:2] * field[5:6] + xyz[2:3] * field[6:7]

    def each_own(step):
        def one(c, carry):
            step(c // cyl + 1, c % cyl + 1)
            return carry

        lax.fori_loop(0, cells, one, 0, unroll=4)

    def each_halo(step):
        def across(j, carry):
            step(0, j)
            step(cxl + 1, j)
            return carry

        def beside_it(i, carry):
            step(i, 0)
            step(i, cyl + 1)
            return carry

        lax.fori_loop(0, nyp, across, 0, unroll=2)
        lax.fori_loop(1, cxl + 1, beside_it, 0, unroll=2)

    def geo_tables(pad, each):
        def step(i, j):
            p = i * nyp + j
            field, xyz = geometry(pad, i, j)
            square = jnp.sum(xyz * xyz, axis=0, keepdims=True)
            to = jnp.where(row8 < 3, xyz, jnp.where(row8 == 3, 1.0 - square, jnp.where(row8 == 4, -1.0, 0.0)))
            by = jnp.where(row8 < 3, 2.0 * xyz, jnp.where(row8 == 3, 1.0, jnp.where(row8 == 4, square, 0.0)))
            th, tm, tl = split3(to)
            bh, bm, bl = split3(by)
            right[p] = jnp.concatenate([th, tm, th, tm, tl, th], axis=0).astype(BF16)
            turned = jnp.concatenate([bh, bh, bm, bm, bh, bl] + [jnp.zeros((8, cell), F32)] * 10, axis=0)
            left[p] = jnp.transpose(turned)[:, :48].astype(BF16)

        each(step)

    def load_tables(pad, each):
        def step(i, j):
            p = i * nyp + j
            field, xyz = geometry(pad, i, j)
            live, press = field[3:4], 2.0 * (field[7:8] - 1.0)
            flat = jnp.where(row8 < 3, xyz, jnp.where(row8 == 3, 1.0, jnp.where(row8 == 7, along(field, xyz), field)))
            flat = flat * live
            pressed = jnp.where(row8 < 4, flat, 0.0) * press
            fh, fm, fl = split3(flat)
            ph, pm, pm2 = split3(pressed)
            loads[p] = jnp.concatenate([fh, ph, fm, pm, fl, pm2], axis=0).astype(BF16)

        each(step)

    chunk = 64

    def weights():
        def step(own_cell, carry):
            here = (own_cell // cyl + 1) * nyp + own_cell % cyl + 1
            for k, (a, b) in enumerate(DIRS):
                there = here + a * nyp + b
                for s in range(cell // chunk):
                    part = pl.ds(s * chunk, chunk)
                    close = jnp.maximum(dot(left[there, part, :], right[here]), 0.0)
                    weight = close * close
                    high = weight.astype(BF16)
                    whigh[own_cell * 9 + k, part, :] = high
                    if (a, b) == (0, 0):
                        wlow[own_cell, part, :] = (weight - high.astype(F32)).astype(BF16)
            return carry

        lax.fori_loop(0, cells, step, 0)

    def forces():
        def step(own_cell, carry):
            here = (own_cell // cyl + 1) * nyp + own_cell % cyl + 1
            total = jnp.zeros((48, cell), F32)
            for k, (a, b) in enumerate(DIRS):
                there = here + a * nyp + b
                summed = dot(loads[there], whigh[own_cell * 9 + k])
                if (a, b) == (0, 0):
                    total = total + (summed + dot(loads[there], wlow[own_cell]))
                else:
                    total = total + summed * alive[k, pl.ds(own_cell, 1), :]
            total = total[0:16] + total[16:32] + total[32:48]
            for c in range(12):
                totals[c, pl.ds(own_cell, 1), :] = total[c : c + 1]
            return carry

        lax.fori_loop(0, cells, step, 0, unroll=2)
        live, press = liveS[...], 2.0 * (rhoS[...] - 1.0)
        count, pressure = totals[3], totals[11]
        own_cell = iota((cells, cell), 0)
        spot = [
            posS[0] + (own_cell // cyl - 2).astype(F32),
            posS[1] + (own_cell % cyl - 2).astype(F32),
            posS[2] - 0.5,
        ]
        rate = (spot[0] * velS[0] + spot[1] * velS[1] + spot[2] * velS[2]) * count + totals[7]
        for c in range(3):
            push = press * (spot[c] * count - totals[c]) + spot[c] * pressure - totals[8 + c]
            push = push - 0.5 * (velS[c] * count - totals[4 + c])
            forS[c] = push * live
            rate = rate - velS[c] * totals[c] - spot[c] * totals[4 + c]
        forS[3] = rate * live

    def advance():
        for c in range(3):
            velS[c] = velS[c] + 0.5 * (0.02 * forS[c] + pushS[c])
        rhoS[...] = rhoS[...] + 0.5 * 0.02 * forS[3]

    springs(disp_ref)
    geo_tables(pad1, each_own)
    load_tables(pad1, each_own)
    for copy in wins:
        copy.wait_recv()
    wall(win1, msg1, 0)
    for copy in halos:
        copy.wait_recv()
    geo_tables(pad1, each_halo)
    load_tables(pad1, each_halo)
    weights()
    forces()
    advance()
    fill_pad(pad2)
    halos2 = halo_copies(pad2, 1)
    for copy in halos2:
        copy.start()
    shell_step(msg1, 0, svel_ref, disp_ref)
    to_rows(speed_out, win2, 1)
    wins2 = win_copies(win2, 1)
    for copy in wins2:
        copy.start()
    springs(offset_out)
    load_tables(pad2, each_own)
    for copy in wins2:
        copy.wait_recv()
    wall(win2, msg2, 1)
    for copy in halos2:
        copy.wait_recv()
    load_tables(pad2, each_halo)
    forces()
    advance()
    for i in range(cxl):
        rows = pl.ds(i * cyl, cyl)
        for c in range(3):
            vel_out[c, i] = velS[c, rows, :]
        rho_out[i] = rhoS[rows, :]
    shell_step(msg2, 1, speed_out, offset_out)
    for copy in wins + halos + wins2 + halos2:
        copy.wait_send()
    for at, msg in enumerate((msg1, msg2)):
        for k, (a, b) in enumerate(peers):
            msg_copy(msg, at, k, a, b, slot_of(a, b)).wait_send()


def body(nx, ny, positions, velocity, density, cell_fill, pair_cells, pair_counts,
         shell_nodes, shell_weights, shell_links, shell_disp, shell_vel):
    cxl, cyl, cell = density.shape
    cells, pads = cxl * cyl, (cxl + 2) * (cyl + 2)
    nodes = shell_vel.shape[1]
    nhi = nodes // LANES
    entries = shell_nodes.size
    ties = jnp.stack([shell_nodes.reshape(-1).astype(F32), shell_weights.reshape(-1)])
    ties = jnp.pad(ties, ((0, 6), (0, LANES - entries)))
    npeers = 3 * ny
    vmem = pl.BlockSpec(memory_space=pltpu.VMEM)
    smem = pl.BlockSpec(memory_space=pltpu.SMEM)
    return pl.pallas_call(
        functools.partial(kernel, nx, ny),
        out_shape=[
            jax.ShapeDtypeStruct(velocity.shape, F32),
            jax.ShapeDtypeStruct(density.shape, F32),
            jax.ShapeDtypeStruct(shell_vel.shape, F32),
            jax.ShapeDtypeStruct(shell_disp.shape, F32),
        ],
        in_specs=[vmem, vmem, vmem, smem, vmem, smem, vmem, vmem, vmem, vmem],
        out_specs=[vmem] * 4,
        scratch_shapes=[
            pltpu.VMEM((3, cells, cell), F32),
            pltpu.VMEM((3, cells, cell), F32),
            pltpu.VMEM((cells, cell), F32),
            pltpu.VMEM((cells, cell), F32),
            pltpu.VMEM((3, cells, cell), F32),
            pltpu.VMEM((4, cells, cell), F32),
            pltpu.VMEM((cxl + 2, cyl + 2, 8, cell), F32),
            pltpu.VMEM((cxl + 2, cyl + 2, 8, cell), F32),
            pltpu.VMEM((3, 3 * nhi, LANES), F32),
            pltpu.VMEM((3, 3 * nhi, LANES), F32),
            pltpu.VMEM((npeers, 8, LANES), F32),
            pltpu.VMEM((npeers, 8, LANES), F32),
            pltpu.VMEM((9, cells, cell), F32),
            pltpu.VMEM((3 * nhi, LANES), F32),
            pltpu.VMEM((3 * nhi, 3 * LANES), BF16),
            pltpu.VMEM((3, nodes), F32),
            pltpu.VMEM((3, nodes), F32),
            pltpu.VMEM((pads, cell, 48), BF16),
            pltpu.VMEM((pads, 48, cell), BF16),
            pltpu.VMEM((pads, 48, cell), BF16),
            pltpu.VMEM((cells * 9, cell, cell), BF16),
            pltpu.VMEM((cells, cell, cell), BF16),
            pltpu.VMEM((12, cells, cell), F32),
            pltpu.SemaphoreType.DMA((2, 8)),
            pltpu.SemaphoreType.DMA((2, 8)),
            pltpu.SemaphoreType.DMA((2, 2)),
            pltpu.SemaphoreType.DMA((2, 2)),
            pltpu.SemaphoreType.DMA((2, npeers)),
            pltpu.SemaphoreType.DMA((2, npeers)),
        ],
        compiler_params=pltpu.CompilerParams(
            collective_id=0, has_side_effects=True, vmem_limit_bytes=56 * 1024 * 1024
        ),
        name="hydro",
    )(positions, velocity, density, cell_fill, pair_cells[0, 0], pair_counts[0], ties,
      shell_links, shell_disp, shell_vel)


def solution(mesh):
    nx, ny = mesh.shape["gx"], mesh.shape["gy"]
    return jax.shard_map(
        functools.partial(body, nx, ny),
        mesh=mesh,
        in_specs=(
            P(None, "gx", "gy", None),
            P(None, "gx", "gy", None),
            P("gx", "gy", None),
            P("gx", "gy"),
            P("gx", "gy", None, None),
            P("gx", "gy", None),
            P(None, "gx", "gy"),
            P(None, "gx", "gy"),
            P(None, "gx"),
            P(None, "gx"),
            P(None, "gx"),
        ),
        out_specs=(P(None, "gx", "gy", None), P("gx", "gy", None), P(None, "gx"), P(None, "gx")),
        check_vma=False,
    )
```

```python
import functools

import jax
import jax.numpy as jnp
from jax import lax
from jax.experimental import pallas as pl
from jax.experimental.pallas import tpu as pltpu
from jax.sharding import PartitionSpec as P

F32 = jnp.float32
BF16 = jnp.bfloat16
MESH = pl.DeviceIdType.MESH
LANES = 128
DIRS = [(a, b) for a in (-1, 0, 1) for b in (-1, 0, 1)]


def iota(shape, dim):
    return lax.broadcasted_iota(jnp.int32, shape, dim)


def split3(value):
    high = value.astype(BF16).astype(F32)
    rest = value - high
    mid = rest.astype(BF16).astype(F32)
    low = (rest - mid).astype(BF16).astype(F32)
    return high, mid, low


def dot(a, b):
    return jnp.dot(a, b, preferred_element_type=F32)


def dot_t(a, b):
    return lax.dot_general(a, b, (((1,), (1,)), ((), ())), preferred_element_type=F32)


def table_of(rows):
    return jnp.concatenate(split3(rows), axis=1).astype(BF16)


def kernel(
    nx, ny,
    pos_ref, vel_ref, rho_ref, fill_ref, pairs_ref, counts_ref, ties_ref, links_ref, disp_ref, svel_ref,
    vel_out, rho_out, speed_out, offset_out,
    posS, velS, rhoS, liveS, pushS, forS, pad1, pad2, win1, win2, msg1, msg2,
    alive, dtab, dtable, beside, node, left, right, loads, whigh, wlow, totals,
    halo_send, halo_recv, win_send, win_recv, msg_send, msg_recv,
):
    cxl, cyl, cell = rho_ref.shape
    cells = cxl * cyl
    nyp = cyl + 2
    nodes = svel_ref.shape[1]
    nhi = nodes // LANES
    ties = 4 * cells
    x, y = lax.axis_index("gx"), lax.axis_index("gy")

    def peer(a, b):
        return (lax.rem(x + a + nx, nx), lax.rem(y + b + ny, ny))

    def slot_of(a, b):
        return (a + 1) * ny + lax.rem(y + b + ny, ny)

    peers = [(a, b) for a in (-1, 0, 1) for b in range(ny) if (a, b) != (0, 0)]
    barrier = pltpu.get_barrier_semaphore()
    for a, b in peers:
        pl.semaphore_signal(barrier, inc=1, device_id=peer(a, b), device_id_type=MESH)

    lane_cell = iota((1, cell), 1)
    for i in range(cxl):
        rows = pl.ds(i * cyl, cyl)
        for c in range(3):
            posS[c, rows, :] = pos_ref[c, i]
            velS[c, rows, :] = vel_ref[c, i]
        rhoS[rows, :] = rho_ref[i]
        for j in range(cyl):
            liveS[pl.ds(i * cyl + j, 1), :] = jnp.where(lane_cell < fill_ref[i, j], 1.0, 0.0).astype(F32)

    def fill_pad(pad):
        def row(i, carry):
            for j in range(cyl):
                one = pl.ds(i * cyl + j, 1)
                for c in range(3):
                    pad[i + 1, j + 1, c : c + 1, :] = posS[c, one, :]
                    pad[i + 1, j + 1, 4 + c : 5 + c, :] = velS[c, one, :]
                pad[i + 1, j + 1, 3:4, :] = liveS[one, :]
                pad[i + 1, j + 1, 7:8, :] = rhoS[one, :]
            return carry

        lax.fori_loop(0, cxl, row, 0, unroll=True)

    def to_rows(source, target, index):
        def step(h, carry):
            at = pl.ds(pl.multiple_of(h * LANES, LANES), LANES)
            for c in range(3):
                if index is None:
                    target[pl.ds(c * nhi + h, 1), :] = source[c : c + 1, at]
                else:
                    target[index, pl.ds(c * nhi + h, 1), :] = source[c : c + 1, at]
            return carry

        lax.fori_loop(0, nhi, step, 0, unroll=8)

    def halo_copies(pad, at):
        def cut(d, size):
            if d == 0:
                return pl.ds(1, size), pl.ds(1, size)
            return (pl.ds(size, 1), pl.ds(0, 1)) if d > 0 else (pl.ds(1, 1), pl.ds(size + 1, 1))

        out = []
        for k, (a, b) in enumerate([d for d in DIRS if d != (0, 0)]):
            (sx, tx), (sy, ty) = cut(a, cxl), cut(b, cyl)
            out.append(
                pltpu.make_async_remote_copy(
                    src_ref=pad.at[sx, sy], dst_ref=pad.at[tx, ty],
                    send_sem=halo_send.at[at, k], recv_sem=halo_recv.at[at, k],
                    device_id=peer(a, b), device_id_type=MESH,
                )
            )
        return out

    def win_copies(win, at):
        return [
            pltpu.make_async_remote_copy(
                src_ref=win.at[1], dst_ref=win.at[1 - a],
                send_sem=win_send.at[at, k], recv_sem=win_recv.at[at, k],
                device_id=peer(a, 0), device_id_type=MESH,
            )
            for k, a in enumerate((-1, 1))
        ]

    def msg_copy(msg, at, k, a, b, slot):
        return pltpu.make_async_remote_copy(
            src_ref=msg.at[ny + y], dst_ref=msg.at[slot],
            send_sem=msg_send.at[at, k], recv_sem=msg_recv.at[at, slot],
            device_id=peer(a, b), device_id_type=MESH,
        )

    fill_pad(pad1)
    to_rows(svel_ref, win1, 1)
    pl.semaphore_wait(barrier, len(peers))
    wins = win_copies(win1, 0)
    for copy in wins:
        copy.start()
    halos = halo_copies(pad1, 0)
    for copy in halos:
        copy.start()

    slots = pairs_ref.shape[1]
    own = iota((cells, slots), 0)
    here = (own // cyl + 1) * nyp + own % cyl + 1
    listed = iota((cells, slots), 1) < counts_ref[0, 1]
    first, second = pairs_ref[0:1, :], pairs_ref[1:2, :]
    for k, (a, b) in enumerate(DIRS):
        if (a, b) == (0, 0):
            alive[k] = jnp.ones((cells, cell), F32)
            continue
        there = here + a * nyp + b
        found = ((first == here) & (second == there)) | ((first == there) & (second == here))
        count = jnp.sum(jnp.where(found & listed, 1.0, 0.0).astype(F32), axis=1, keepdims=True)
        alive[k] = jnp.broadcast_to(count, (cells, cell))

    block = 512

    def springs(disp):
        to_rows(disp, dtab, None)
        dtable[...] = table_of(dtab[...])

        def step(j, carry):
            at = pl.ds(pl.multiple_of(j * block, block), block)
            sums = [jnp.zeros((nhi, block), F32) for c in range(3)]
            for l in range(links_ref.shape[0]):
                index = links_ref[l : l + 1, at]
                low, high = index & (LANES - 1), index >> 7
                hot = jnp.where(iota((LANES, block), 0) == low, 1.0, 0.0).astype(BF16)
                got = dot(dtable[...], jnp.concatenate([hot, hot, hot], axis=0))
                at_high = iota((nhi, block), 0) == high
                for c in range(3):
                    sums[c] = sums[c] + jnp.where(at_high, got[c * nhi : (c + 1) * nhi], 0.0)
            for c in range(3):
                beside[c : c + 1, at] = jnp.sum(sums[c], axis=0, keepdims=True)
            return carry

        lax.fori_loop(0, nodes // block, step, 0, unroll=2)

    id_row, weight_row = ties_ref[0:1, :], ties_ref[1:2, :]
    diag = iota((ties, LANES), 0) == iota((ties, LANES), 1)
    id_col = jnp.sum(jnp.where(diag, id_row, 0.0), axis=1, keepdims=True)
    weight_col = jnp.sum(jnp.where(diag, weight_row, 0.0), axis=1, keepdims=True)

    def wall(win, msg, at):
        place = id_col.astype(jnp.int32) - (x - 1) * nodes
        low, high = place & (LANES - 1), place >> 7
        hot = jnp.where(iota((ties, LANES), 1) == low, 1.0, 0.0).astype(BF16)
        hot = jnp.concatenate([hot, hot, hot], axis=1)
        value = [jnp.zeros((ties, 1), F32) for c in range(3)]
        lane = iota((ties, 3 * nhi), 1)
        for strip in range(3):
            got = dot_t(hot, table_of(win[strip]))
            inside = high - strip * nhi
            fits = (inside >= 0) & (inside < nhi)
            for c in range(3):
                pick = fits & (lane == inside + c * nhi)
                value[c] = value[c] + jnp.sum(jnp.where(pick, got, 0.0), axis=1, keepdims=True)
        contact = jnp.maximum(1.0 - 2.0 * posS[2], 0.0)
        contact = contact * contact * liveS[...]
        mine = ny + y
        msg[mine] = jnp.zeros((8, LANES), F32)
        spread = iota((cells, LANES), 0) == (iota((cells, LANES), 1) & (cells - 1))
        for c in range(3):
            tied = value[c] * weight_col
            coupled = sum(tied[k * cells : (k + 1) * cells] for k in range(4))
            push = 0.2 * contact * (coupled - velS[c])
            if c == 2:
                push = push + 0.1 * contact
            pushS[c] = push
            load = -jnp.sum(push, axis=1, keepdims=True)
            row = jnp.sum(jnp.where(spread, load, 0.0), axis=0, keepdims=True)
            msg[mine, c : c + 1, :] = row * weight_row
        msg[mine, 3:4, :] = id_row
        for k, (a, b) in enumerate(peers):
            msg_copy(msg, at, k, a, b, (1 - a) * ny + y).start()

    def shell_step(msg, at, speed, disp):
        for k, (a, b) in enumerate(peers):
            msg_copy(msg, at, k, a, b, slot_of(a, b)).wait_recv()

        def add(s, total):
            note = msg[s]
            place = note[3:4].astype(jnp.int32) - x * nodes
            low, high = place & (LANES - 1), place >> 7
            at_high = iota((nhi, LANES), 0) == high
            share = jnp.concatenate([jnp.where(at_high, note[c : c + 1], 0.0) for c in range(3)], axis=0)
            hot = jnp.where(iota((LANES, LANES), 0) == low, 1.0, 0.0).astype(BF16)
            return total + dot_t(table_of(share), jnp.concatenate([hot, hot, hot], axis=1))

        dtab[...] = lax.fori_loop(0, 3 * ny, add, jnp.zeros((3 * nhi, LANES), F32), unroll=True)

        def row(h, carry):
            for c in range(3):
                node[c : c + 1, pl.ds(pl.multiple_of(h * LANES, LANES), LANES)] = dtab[pl.ds(c * nhi + h, 1), :]
            return carry

        lax.fori_loop(0, nhi, row, 0, unroll=8)
        old = disp[...]
        spring = 4.0 * old - beside[...]
        new = speed[...] + 0.5 * (0.2 * node[...] - 0.5 * spring)
        speed_out[...] = new
        offset_out[...] = old + 0.5 * new

    row8 = iota((8, cell), 0)

    def geometry(pad, i, j):
        field = pad[i, j]
        shift_x = (i - 3).astype(F32) if not isinstance(i, int) else float(i - 3)
        shift_y = (j - 3).astype(F32) if not isinstance(j, int) else float(j - 3)
        shift = jnp.where(row8 == 0, shift_x, jnp.where(row8 == 1, shift_y, -0.5))
        xyz = jnp.where(row8 < 3, field + shift, 0.0)
        return field, xyz

    def along(field, xyz):
        return xyz[0:1] * field[4:5] + xyz[1:2] * field[5:6] + xyz[2:3] * field[6:7]

    def each_own(step):
        def one(c, carry):
            step(c // cyl + 1, c % cyl + 1)
            return carry

        lax.fori_loop(0, cells, one, 0, unroll=4)

    def each_halo(step):
        def across(j, carry):
            step(0, j)
            step(cxl + 1, j)
            return carry

        def beside_it(i, carry):
            step(i, 0)
            step(i, cyl + 1)
            return carry

        lax.fori_loop(0, nyp, across, 0, unroll=2)
        lax.fori_loop(1, cxl + 1, beside_it, 0, unroll=2)

    def geo_tables(pad, each):
        def step(i, j):
            p = i * nyp + j
            field, xyz = geometry(pad, i, j)
            square = jnp.sum(xyz * xyz, axis=0, keepdims=True)
            to = jnp.where(row8 < 3, xyz, jnp.where(row8 == 3, 1.0 - square, jnp.where(row8 == 4, -1.0, 0.0)))
            by = jnp.where(row8 < 3, 2.0 * xyz, jnp.where(row8 == 3, 1.0, jnp.where(row8 == 4, square, 0.0)))
            th, tm, tl = split3(to)
            bh, bm, bl = split3(by)
            right[p] = jnp.concatenate([th, tm, th, tm, tl, th], axis=0).astype(BF16)
            turned = jnp.concatenate([bh, bh, bm, bm, bh, bl] + [jnp.zeros((8, cell), F32)] * 10, axis=0)
            left[p] = jnp.transpose(turned)[:, :48].astype(BF16)

        each(step)

    def load_tables(pad, each):
        def step(i, j):
            p = i * nyp + j
            field, xyz = geometry(pad, i, j)
            live, press = field[3:4], 2.0 * (field[7:8] - 1.0)
            flat = jnp.where(row8 < 3, xyz, jnp.where(row8 == 3, 1.0, jnp.where(row8 == 7, along(field, xyz), field)))
            flat = flat * live
            pressed = jnp.where(row8 < 4, flat, 0.0) * press
            fh, fm, fl = split3(flat)
            ph, pm, pm2 = split3(pressed)
            loads[p] = jnp.concatenate([fh, ph, fm, pm, fl, pm2], axis=0).astype(BF16)

        each(step)

    chunk = 64

    def weights():
        def step(own_cell, carry):
            here = (own_cell // cyl + 1) * nyp + own_cell % cyl + 1
            for k, (a, b) in enumerate(DIRS):
                there = here + a * nyp + b
                for s in range(cell // chunk):
                    part = pl.ds(s * chunk, chunk)
                    close = jnp.maximum(dot(left[there, part, :], right[here]), 0.0)
                    weight = close * close
                    high = weight.astype(BF16)
                    whigh[own_cell * 9 + k, part, :] = high
                    if (a, b) == (0, 0):
                        wlow[own_cell, part, :] = (weight - high.astype(F32)).astype(BF16)
            return carry

        lax.fori_loop(0, cells, step, 0, unroll=2)

    def forces():
        def step(own_cell, carry):
            here = (own_cell // cyl + 1) * nyp + own_cell % cyl + 1
            total = jnp.zeros((48, cell), F32)
            for k, (a, b) in enumerate(DIRS):
                there = here + a * nyp + b
                summed = dot(loads[there], whigh[own_cell * 9 + k])
                if (a, b) == (0, 0):
                    total = total + (summed + dot(loads[there], wlow[own_cell]))
                else:
                    total = total + summed * alive[k, pl.ds(own_cell, 1), :]
            total = total[0:16] + total[16:32] + total[32:48]
            for c in range(12):
                totals[c, pl.ds(own_cell, 1), :] = total[c : c + 1]
            return carry

        lax.fori_loop(0, cells, step, 0, unroll=4)
        live, press = liveS[...], 2.0 * (rhoS[...] - 1.0)
        count, pressure = totals[3], totals[11]
        own_cell = iota((cells, cell), 0)
        spot = [
            posS[0] + (own_cell // cyl - 2).astype(F32),
            posS[1] + (own_cell % cyl - 2).astype(F32),
            posS[2] - 0.5,
        ]
        rate = (spot[0] * velS[0] + spot[1] * velS[1] + spot[2] * velS[2]) * count + totals[7]
        for c in range(3):
            push = press * (spot[c] * count - totals[c]) + spot[c] * pressure - totals[8 + c]
            push = push - 0.5 * (velS[c] * count - totals[4 + c])
            forS[c] = push * live
            rate = rate - velS[c] * totals[c] - spot[c] * totals[4 + c]
        forS[3] = rate * live

    def advance():
        for c in range(3):
            velS[c] = velS[c] + 0.5 * (0.02 * forS[c] + pushS[c])
        rhoS[...] = rhoS[...] + 0.5 * 0.02 * forS[3]

    springs(disp_ref)
    for copy in wins:
        copy.wait_recv()
    wall(win1, msg1, 0)
    for copy in halos:
        copy.wait_recv()
    geo_tables(pad1, each_own)
    load_tables(pad1, each_own)
    geo_tables(pad1, each_halo)
    load_tables(pad1, each_halo)
    weights()
    forces()
    advance()
    fill_pad(pad2)
    halos2 = halo_copies(pad2, 1)
    for copy in halos2:
        copy.start()
    shell_step(msg1, 0, svel_ref, disp_ref)
    to_rows(speed_out, win2, 1)
    wins2 = win_copies(win2, 1)
    for copy in wins2:
        copy.start()
    springs(offset_out)
    for copy in wins2:
        copy.wait_recv()
    wall(win2, msg2, 1)
    for copy in halos2:
        copy.wait_recv()
    load_tables(pad2, each_own)
    load_tables(pad2, each_halo)
    forces()
    advance()
    for i in range(cxl):
        rows = pl.ds(i * cyl, cyl)
        for c in range(3):
            vel_out[c, i] = velS[c, rows, :]
        rho_out[i] = rhoS[rows, :]
    shell_step(msg2, 1, speed_out, offset_out)
    for copy in wins + halos + wins2 + halos2:
        copy.wait_send()
    for at, msg in enumerate((msg1, msg2)):
        for k, (a, b) in enumerate(peers):
            msg_copy(msg, at, k, a, b, slot_of(a, b)).wait_send()


def body(nx, ny, positions, velocity, density, cell_fill, pair_cells, pair_counts,
         shell_nodes, shell_weights, shell_links, shell_disp, shell_vel):
    cxl, cyl, cell = density.shape
    cells, pads = cxl * cyl, (cxl + 2) * (cyl + 2)
    nodes = shell_vel.shape[1]
    nhi = nodes // LANES
    entries = shell_nodes.size
    ties = jnp.stack([shell_nodes.reshape(-1).astype(F32), shell_weights.reshape(-1)])
    ties = jnp.pad(ties, ((0, 6), (0, LANES - entries)))
    npeers = 3 * ny
    vmem = pl.BlockSpec(memory_space=pltpu.VMEM)
    smem = pl.BlockSpec(memory_space=pltpu.SMEM)
    return pl.pallas_call(
        functools.partial(kernel, nx, ny),
        out_shape=[
            jax.ShapeDtypeStruct(velocity.shape, F32),
            jax.ShapeDtypeStruct(density.shape, F32),
            jax.ShapeDtypeStruct(shell_vel.shape, F32),
            jax.ShapeDtypeStruct(shell_disp.shape, F32),
        ],
        in_specs=[vmem, vmem, vmem, smem, vmem, smem, vmem, vmem, vmem, vmem],
        out_specs=[vmem] * 4,
        scratch_shapes=[
            pltpu.VMEM((3, cells, cell), F32),
            pltpu.VMEM((3, cells, cell), F32),
            pltpu.VMEM((cells, cell), F32),
            pltpu.VMEM((cells, cell), F32),
            pltpu.VMEM((3, cells, cell), F32),
            pltpu.VMEM((4, cells, cell), F32),
            pltpu.VMEM((cxl + 2, cyl + 2, 8, cell), F32),
            pltpu.VMEM((cxl + 2, cyl + 2, 8, cell), F32),
            pltpu.VMEM((3, 3 * nhi, LANES), F32),
            pltpu.VMEM((3, 3 * nhi, LANES), F32),
            pltpu.VMEM((npeers, 8, LANES), F32),
            pltpu.VMEM((npeers, 8, LANES), F32),
            pltpu.VMEM((9, cells, cell), F32),
            pltpu.VMEM((3 * nhi, LANES), F32),
            pltpu.VMEM((3 * nhi, 3 * LANES), BF16),
            pltpu.VMEM((3, nodes), F32),
            pltpu.VMEM((3, nodes), F32),
            pltpu.VMEM((pads, cell, 48), BF16),
            pltpu.VMEM((pads, 48, cell), BF16),
            pltpu.VMEM((pads, 48, cell), BF16),
            pltpu.VMEM((cells * 9, cell, cell), BF16),
            pltpu.VMEM((cells, cell, cell), BF16),
            pltpu.VMEM((12, cells, cell), F32),
            pltpu.SemaphoreType.DMA((2, 8)),
            pltpu.SemaphoreType.DMA((2, 8)),
            pltpu.SemaphoreType.DMA((2, 2)),
            pltpu.SemaphoreType.DMA((2, 2)),
            pltpu.SemaphoreType.DMA((2, npeers)),
            pltpu.SemaphoreType.DMA((2, npeers)),
        ],
        compiler_params=pltpu.CompilerParams(
            collective_id=0, has_side_effects=True, vmem_limit_bytes=56 * 1024 * 1024
        ),
        name="hydro",
    )(positions, velocity, density, cell_fill, pair_cells[0, 0], pair_counts[0], ties,
      shell_links, shell_disp, shell_vel)


def solution(mesh):
    nx, ny = mesh.shape["gx"], mesh.shape["gy"]
    return jax.shard_map(
        functools.partial(body, nx, ny),
        mesh=mesh,
        in_specs=(
            P(None, "gx", "gy", None),
            P(None, "gx", "gy", None),
            P("gx", "gy", None),
            P("gx", "gy"),
            P("gx", "gy", None, None),
            P("gx", "gy", None),
            P(None, "gx", "gy"),
            P(None, "gx", "gy"),
            P(None, "gx"),
            P(None, "gx"),
            P(None, "gx"),
        ),
        out_specs=(P(None, "gx", "gy", None), P("gx", "gy", None), P(None, "gx"), P(None, "gx")),
        check_vma=False,
    )
```
